32 devices in a mesh: groups: 2 (over x), frames: 16 (over z, y, core).
Axes of the slice: x: 2, y: 2, z: 4, core: 2. Of those that a mesh axis runs over, the one named last changes fastest.
Arguments:
- video: float32 [4, 16, 256, 256], P('groups', 'frames'), parts along dimension 0, may hold values from -9 to 9
- clip_start: int32 [4], P('groups'), parts along dimension 0, may hold values from 0 to 7
- gain_space: float32 [256], replicated, may hold values from 0.1 to 1.9
- qkv_space: float32 [256, 768], replicated, may hold values from -0.375 to 0.375
- out_space: float32 [256, 256], replicated, may hold values from -0.375 to 0.375
- gain_time: float32 [256], replicated, may hold values from 0.1 to 1.9
- qkv_time: float32 [256, 768], replicated, may hold values from -0.375 to 0.375
- out_time: float32 [256, 256], replicated, may hold values from -0.375 to 0.375
- code_sums: float32 [8192, 256], P(('groups', 'frames')), parts along dimension 0, may hold values from -12 to 12
- code_counts: float32 [8192], P(('groups', 'frames')), parts along dimension 0, may hold values from 1 to 10
Outputs:
- latents: float32 [4, 16, 256, 256], P('groups', None, 'frames'), parts along dimension 0
- new_sums: float32 [8192, 256], P(('groups', 'frames')), parts along dimension 0
- new_counts: float32 [8192], P(('groups', 'frames')), parts along dimension 0
- new_codebook: float32 [8192, 256], P(('groups', 'frames')), parts along dimension 0
The draws below stay inside these ranges and needn't reach their ends.
There are 2 independent parts, one for each index of `groups`. The reference program is written for one: setup_inputs(seed, part) draws one part's arguments, and reference() takes and returns one part's arrays. A program takes and returns all parts, laid end to end along the dimension named above; an argument that names none is the same for every part. Nothing has to cross between parts.
All inputs are finite; a program needn't handle non-finite values.
Results may differ from the reference program's by a relative error of at most 0.0003.
Values sent between devices are 32-bit elements; how exact they have to be, the bound alone decides.
No kernel may reach another device: no remote copies, remote signals or barrier semaphores. Data moves between devices by JAX's collectives and lax.ppermute only.
A program may use at most 64 MiB of HBM per device.

```python
import math
import jax
import jax.numpy as jnp
from jax import lax

D = 256
HEADS = 4
HW = 256
K = 4096
CLIPS = 2
FRAMES = 16


def centre_count():
    return max(K // 16, 2)


def centre_rows(key):
    return jax.random.truncated_normal(jax.random.fold_in(key, 7001), -4.0, 4.0, (centre_count(), D), jnp.float32)


def draw_video(key, part):
    centres = centre_rows(key)
    shape_tok = (CLIPS, FRAMES, HW)
    first_pick = jax.random.randint(jax.random.fold_in(key, 7002), shape_tok, 0, centre_count())
    second_pick = jax.random.randint(jax.random.fold_in(key, 7003), shape_tok, 0, centre_count())
    chosen = jnp.minimum(first_pick, second_pick)
    picked = jnp.take(centres, chosen, axis=0)
    amplitude = 1.2
    noise = 0.9 * jax.random.truncated_normal(jax.random.fold_in(key, 7004), -4.0, 4.0, shape_tok + (D,), jnp.float32)
    return (amplitude * picked + noise).astype(jnp.float32)


def draw_code_sums(key, part):
    centres = centre_rows(key)
    owner = jax.random.permutation(jax.random.fold_in(key, 7006), jnp.arange(K, dtype=jnp.int32)) % centre_count()
    picked = jnp.take(centres, owner, axis=0)
    row_scale = jax.random.uniform(jax.random.fold_in(key, 7007), (K, 1), jnp.float32, 0.5, 1.5)
    noise = 0.8 * jax.random.truncated_normal(jax.random.fold_in(key, 7008), -4.0, 4.0, (K, D), jnp.float32)
    return (row_scale * (picked + noise)).astype(jnp.float32)


def block_scale(key, shape, pieces, low, top_value):
    def one(dim, parts):
        draws = jax.random.uniform(jax.random.fold_in(jax.random.fold_in(key, 6), dim), (parts,), jnp.float32, low / len(pieces), top_value / len(pieces))
        return jnp.repeat(jnp.exp(draws), shape[dim] // parts).reshape((-1,) + (1,) * (len(shape) - dim - 1))

    loudness = one(*pieces[0])
    for cut in pieces[1:]:
        loudness = loudness * one(*cut)
    return loudness


def normal_values(rng, shape, scale, reach, held_as=jnp.bfloat16):
    drawn = jax.random.normal(rng, shape, jnp.float32) * scale
    return jnp.minimum(jnp.maximum(drawn, -reach), reach).astype(held_as)


def setup_inputs(seed: int = 0, part: int = 0) -> dict:
    keys = jax.random.split(jax.random.key(seed), 11)
    part_keys = jax.random.split(jax.random.fold_in(keys[10], part), 11)
    return {
        "video": draw_video(jax.random.fold_in(jax.random.fold_in(keys[10], part), 71), part),
        "clip_start": jax.random.randint(part_keys[1], (CLIPS,), 0, FRAMES // 2).astype(jnp.int32),
        "gain_space": jnp.clip(1.0 + 0.18 * jax.random.normal(keys[2], (D,), jnp.float32), 0.1, 1.9),
        "qkv_space": normal_values(keys[3], (D, 3 * D), D ** -0.5, 0.375, jnp.float32),
        "out_space": normal_values(keys[4], (D, D), D ** -0.5, 0.375, jnp.float32),
        "gain_time": jnp.clip(1.0 + 0.18 * jax.random.normal(keys[5], (D,), jnp.float32), 0.1, 1.9),
        "qkv_time": normal_values(keys[6], (D, 3 * D), D ** -0.5, 0.375, jnp.float32),
        "out_time": normal_values(keys[7], (D, D), D ** -0.5, 0.375, jnp.float32),
        "code_sums": draw_code_sums(jax.random.fold_in(jax.random.fold_in(keys[10], part), 71), part),
        "code_counts": jnp.clip(jnp.exp(math.log(10.0) - 2.3025851 * jax.random.uniform(part_keys[9], (K,), jnp.float32) ** block_scale(part_keys[9], (K,), ((0, 16),), -0.2, 0.2)), 1.0, 10.0),
    }


ATTN_SCALE = 10.0
SOFTMAX_WARMTH = 0.05
DECAY_RATE = 0.9
EPSILON = 1e-06
TOP_PRECISION = lax.Precision.HIGHEST

def rms_norm(values, gain_vec):
    return values * lax.rsqrt(lax.optimization_barrier(jnp.mean(values * values, -1, keepdims=True)) + EPSILON) * gain_vec

def unit_vec(values):
    return values * lax.rsqrt(lax.optimization_barrier(jnp.sum(values * values, -1, keepdims=True)) + EPSILON)

def spatial_block(one_frame, gain_vec, w_qkv, w_out):
    width = one_frame.shape[-1]
    normed = rms_norm(one_frame, gain_vec)
    packed = jnp.dot(normed, w_qkv, precision=TOP_PRECISION)
    queries = unit_vec(packed[:, :width].reshape(-1, HEADS, width // HEADS))
    key_vecs = unit_vec(packed[:, width:2 * width].reshape(-1, HEADS, width // HEADS))
    values = packed[:, 2 * width:].reshape(-1, HEADS, width // HEADS)
    scores = ATTN_SCALE * jnp.einsum('qhd,khd->hqk', queries, key_vecs, precision=TOP_PRECISION)
    assignment_weights = jnp.exp(scores)
    totals = lax.optimization_barrier(jnp.sum(assignment_weights, -1)).T[:, :, None]
    mixed = jnp.einsum('hqk,khd->qhd', assignment_weights, values, precision=TOP_PRECISION) / totals
    return one_frame + jnp.dot(mixed.reshape(-1, width), w_out, precision=TOP_PRECISION)

def time_block(spaced, clip_start, gain_vec, w_qkv, w_out):
    clips, frames, places, width = spaced.shape
    normed = rms_norm(spaced, gain_vec)
    packed = jnp.einsum('ctpd,de->ctpe', normed, w_qkv, precision=TOP_PRECISION)
    shape_heads = (clips, frames, places, HEADS, width // HEADS)
    queries = unit_vec(packed[..., :width].reshape(shape_heads))
    key_vecs = unit_vec(packed[..., width:2 * width].reshape(shape_heads))
    values = packed[..., 2 * width:].reshape(shape_heads)
    scores = ATTN_SCALE * jnp.einsum('ctphd,csphd->cphts', queries, key_vecs, precision=TOP_PRECISION)
    later = jnp.arange(frames, dtype=jnp.int32)[:, None]
    earlier = jnp.arange(frames, dtype=jnp.int32)[None, :]
    allowed = (earlier <= later)[None] & ((earlier[None] >= clip_start[:, None, None]) | (earlier == later)[None])
    assignment_weights = jnp.exp(scores) * allowed[:, None, None, :, :].astype(jnp.float32)
    totals = jnp.transpose(lax.optimization_barrier(jnp.sum(assignment_weights, -1)), (0, 3, 1, 2))[..., None]
    mixed = jnp.einsum('cphts,csphd->ctphd', assignment_weights, values, precision=TOP_PRECISION) / totals
    return spaced + jnp.einsum('ctpd,de->ctpe', mixed.reshape(clips, frames, places, width), w_out, precision=TOP_PRECISION)

def reference(video, clip_start, gain_space, qkv_space, out_space, gain_time, qkv_time, out_time, code_sums, code_counts):
    clips, frames, places, width = video.shape
    flat_frames = video.reshape(clips * frames, places, width)
    spaced = lax.map(lambda one_frame: spatial_block(one_frame, gain_space, qkv_space, out_space), flat_frames)
    spaced = spaced.reshape(clips, frames, places, width)
    latents = time_block(spaced, clip_start, gain_time, qkv_time, out_time)
    unit_token_vectors = unit_vec(latents.reshape(clips * frames, places, width))
    unit_code_vectors = unit_vec(code_sums / code_counts[:, None])

    def accumulate(carry, rows_per_block):
        sums_acc, counts_acc = carry
        assignment_weights = jnp.exp(jnp.dot(rows_per_block, unit_code_vectors.T, precision=TOP_PRECISION) / SOFTMAX_WARMTH)
        probs = assignment_weights / lax.optimization_barrier(jnp.sum(assignment_weights, 1, keepdims=True))
        sums_acc = sums_acc + lax.dot_general(probs, rows_per_block, (((0,), (0,)), ((), ())), precision=TOP_PRECISION)
        counts_acc = counts_acc + lax.optimization_barrier(jnp.sum(probs, 0))
        return ((sums_acc, counts_acc), None)
    start_carry = (jnp.zeros(code_sums.shape, jnp.float32), jnp.zeros(code_counts.shape, jnp.float32))
    (term_sums, term_counts), _ = lax.scan(accumulate, start_carry, unit_token_vectors)
    new_sums = DECAY_RATE * code_sums + (1.0 - DECAY_RATE) * term_sums
    new_counts = DECAY_RATE * code_counts + (1.0 - DECAY_RATE) * term_counts
    new_codebook = new_sums / new_counts[:, None]
    return (latents, new_sums, new_counts, new_codebook)
```

```python
import math

import jax
import jax.numpy as jnp
from jax import lax
from jax.experimental import pallas as pl
from jax.experimental.pallas import tpu as pltpu
from jax.sharding import PartitionSpec as P

HEADS = 4
ATTN_SCALE = 10.0
SOFTMAX_WARMTH = 0.05
DECAY_RATE = 0.9
EPSILON = 1e-06
SHARERS = 4
VMEM_BYTES = 40 * 1024 * 1024
BF16 = jnp.bfloat16
F32 = jnp.float32


def params(**kw):
    return pltpu.CompilerParams(vmem_limit_bytes=VMEM_BYTES, **kw)


def split(x):
    high = x.astype(BF16)
    return high, (x - high.astype(F32)).astype(BF16)


def dot(a, b):
    return jnp.dot(a, b, preferred_element_type=F32)


def dot_t(a, b):
    return lax.dot_general(a, b, (((1,), (1,)), ((), ())), preferred_element_type=F32)


def dot3(a, b, product=dot):
    ah, al = a
    bh, bl = b
    return product(ah, bh) + (product(al, bh) + product(ah, bl))


def attend(x, gain, w_qkv, w_out, mask):
    tokens, width = x.shape
    head = width // HEADS
    h = x * lax.rsqrt(jnp.mean(x * x, -1, keepdims=True) + EPSILON) * gain
    packed = dot3(split(h), split(w_qkv))
    row_head = lax.broadcasted_iota(jnp.int32, (width, width), 0) // head
    lane_head = lax.broadcasted_iota(jnp.int32, (width, width), 1) // head
    same_head = (row_head == lane_head).astype(BF16)

    def unit_heads(v):
        high, low = split(v * v)
        return v * lax.rsqrt(dot(high, same_head) + dot(low, same_head) + EPSILON)

    q = split(unit_heads(packed[:, :width]) * ATTN_SCALE)
    k = split(unit_heads(packed[:, width : 2 * width]))
    v = split(packed[:, 2 * width :])
    lanes = lax.broadcasted_iota(jnp.int32, (tokens, width), 1) // head
    mixed = jnp.zeros((tokens, width), F32)
    for i in range(HEADS):
        mine = lanes == i
        qi = [jnp.where(mine, part, jnp.zeros_like(part)) for part in q]
        weights = jnp.exp(dot3(qi, k, dot_t))
        if mask is not None:
            weights = jnp.where(mask, weights, 0.0)
        vi = [jnp.where(mine, part, jnp.full_like(part, fill)) for part, fill in zip(v, (1.0, 0.0))]
        r = dot3(split(weights), vi)
        totals = jnp.concatenate([r[:, width // 2 :], r[:, : width // 2]], axis=1)
        mixed = jnp.where(mine, r / totals, mixed)
    return x + dot3(split(mixed), split(w_out))


def space_kernel(x_ref, gain_ref, w_qkv_ref, w_out_ref, out_ref):
    y = attend(x_ref[0], gain_ref[...], w_qkv_ref[...], w_out_ref[...], None)
    out_ref[...] = y.reshape(out_ref.shape)


def time_kernel(start_ref, x_ref, gain_ref, w_qkv_ref, w_out_ref, latents_ref, unit_ref):
    senders, _, local_frames, places, width = x_ref.shape
    tokens = senders * local_frames * places
    x = x_ref[...].reshape(tokens, width)
    rows = lax.broadcasted_iota(jnp.int32, (tokens, tokens), 0)
    cols = lax.broadcasted_iota(jnp.int32, (tokens, tokens), 1)
    later, earlier = rows // places, cols // places
    start = start_ref[pl.program_id(0)]
    mask = ((rows - later * places) == (cols - earlier * places)) & (
        (earlier == later) | ((earlier < later) & (earlier >= start))
    )
    y = attend(x, gain_ref[...], w_qkv_ref[...], w_out_ref[...], mask)
    latents_ref[...] = y.reshape(latents_ref.shape)
    unit_ref[...] = y * lax.rsqrt(jnp.sum(y * y, -1, keepdims=True) + EPSILON)


def column(row, lanes):
    return jnp.transpose(jnp.broadcast_to(row, (lanes, row.shape[1])))


def code_kernel(sums_ref, counts_ref, out_ref):
    book = sums_ref[...] / column(counts_ref[...], sums_ref.shape[1])
    unit = book * lax.rsqrt(jnp.sum(book * book, -1, keepdims=True) + EPSILON)
    out_ref[...] = unit * (math.log2(math.e) / SOFTMAX_WARMTH)


def score_kernel(*refs, blocks, chunks):
    codes, units = refs[:blocks], refs[blocks : blocks + chunks]
    w_ref, totals_ref = refs[blocks + chunks :]
    rows = codes[0].shape[0]
    for j in range(chunks):
        u = units[j][...].astype(BF16)
        totals = None
        for r in range(blocks):
            high, low = split(codes[r][...])
            w = jnp.exp2(dot_t(high, u) + dot_t(low, u)).astype(BF16)
            w_ref[j, r * rows : (r + 1) * rows, :] = w
            part = jnp.sum(w.astype(F32), 0, keepdims=True)
            totals = part if totals is None else totals + part
        totals_ref[j] = totals


def term_kernel(*refs, blocks, chunks, calls):
    ws, refs = refs[:calls], refs[calls:]
    units, refs = refs[:chunks], refs[chunks:]
    totals, (out_ref,) = refs[: SHARERS * calls], refs[SHARERS * calls :]
    each = chunks // calls
    rows = ws[0].shape[1] // blocks
    width = units[0].shape[1]
    scaled, shares = [], []
    for j in range(chunks):
        total = None
        for m in range(SHARERS):
            source = j ^ m
            part = totals[m * calls + source // each][source % each]
            total = part if total is None else total + part
        share = 1.0 / total
        column_share = column(share, 128)
        column_share = jnp.concatenate([column_share] * (width // 128), axis=1)
        scaled.append((units[j][...] * column_share).astype(BF16))
        high, low = split(share)
        index = lax.broadcasted_iota(jnp.int32, (16, share.shape[1]), 0)
        shares.append(
            jnp.where(index == 0, high.astype(F32), jnp.where(index == 1, low.astype(F32), 0.0)).astype(BF16)
        )
    for r in range(blocks):
        sums = jnp.zeros((rows, width), F32)
        counts = jnp.zeros((16, rows), F32)
        for j in range(chunks):
            w = ws[j // each][j % each, r * rows : (r + 1) * rows, :]
            sums = sums + dot(w, scaled[j])
            counts = counts + dot_t(shares[j], w)
        out_ref[r, :rows, :] = sums
        counts = jnp.sum(counts, 0, keepdims=True)
        if rows < width:
            counts = jnp.concatenate([counts, jnp.zeros((1, width - rows), F32)], axis=1)
        out_ref[r, rows:, :] = jnp.broadcast_to(counts, (8, width))


def update_kernel(*refs, blocks):
    sums_ref, counts_ref = refs[:2]
    terms = refs[2 : 2 + blocks]
    new_sums_ref, new_counts_ref, new_book_ref = refs[2 + blocks :]
    rows, width = sums_ref.shape
    term = terms[0][...]
    for other in terms[1:]:
        term = term + other[...]
    sums = DECAY_RATE * sums_ref[...] + (1.0 - DECAY_RATE) * term[:rows]
    counts = DECAY_RATE * counts_ref[...] + (1.0 - DECAY_RATE) * term[rows : rows + 1, :rows]
    new_sums_ref[...] = sums
    new_counts_ref[...] = counts
    new_book_ref[...] = sums / column(counts, width)


def whole(a):
    return pl.BlockSpec(a.shape, lambda *_: (0,) * a.ndim)


def cost(flops, *arrays):
    return pl.CostEstimate(
        flops=int(flops), bytes_accessed=int(sum(a.size * a.dtype.itemsize for a in arrays)), transcendentals=0
    )


def shape(*dims, dtype=F32):
    return jax.ShapeDtypeStruct(dims, dtype)


def simple_call(kernel, outs, *args, flops=0, name=None):
    return pl.pallas_call(
        kernel,
        out_shape=outs,
        compiler_params=params(),
        cost_estimate=cost(flops, *args, *(outs if isinstance(outs, (tuple, list)) else [outs])),
        name=name,
    )(*args)


def make_local(devices):
    sharers, blocks = SHARERS, devices // SHARERS

    def swap(x, bits):
        return lax.ppermute(x, "frames", [(i, i ^ bits) for i in range(devices)])

    def local(
        video,
        clip_start,
        gain_space,
        qkv_space,
        out_space,
        gain_time,
        qkv_time,
        out_time,
        code_sums,
        code_counts,
    ):
        clips, local_frames, all_places, width = video.shape
        places = all_places // devices
        frames = local_frames * devices
        code_rows = code_sums.shape[0]
        tiles = clips * local_frames
        tokens = frames * places
        flat = video.reshape(tiles, all_places, width)
        gain_space, gain_time = gain_space[None], gain_time[None]
        counts_row = code_counts[None]

        codes = simple_call(code_kernel, shape(code_rows, width), code_sums, counts_row, name="unit_codes")
        code_blocks = [codes] + [swap(codes, r * sharers) for r in range(1, blocks)]

        spaced = pl.pallas_call(
            space_kernel,
            grid=(tiles,),
            in_specs=[
                pl.BlockSpec((1, all_places, width), lambda i: (i, 0, 0)),
                whole(gain_space),
                whole(qkv_space),
                whole(out_space),
            ],
            out_specs=pl.BlockSpec((devices, 1, places, width), lambda i: (0, i, 0, 0)),
            out_shape=shape(devices, tiles, places, width),
            compiler_params=params(),
            cost_estimate=cost(tiles * 4e9, flat, qkv_space),
            name="space_attention",
        )(flat, gain_space, qkv_space, out_space)

        by_place = lax.all_to_all(spaced, "frames", split_axis=0, concat_axis=0, tiled=True)
        by_place = by_place.reshape(devices, clips, local_frames, places, width)

        latents, unit = pl.pallas_call(
            time_kernel,
            grid=(clips,),
            in_specs=[
                pl.BlockSpec(memory_space=pltpu.SMEM),
                pl.BlockSpec((devices, 1, local_frames, places, width), lambda i: (0, i, 0, 0, 0)),
                whole(gain_time),
                whole(qkv_time),
                whole(out_time),
            ],
            out_specs=(
                pl.BlockSpec((1, frames, places, width), lambda i: (i, 0, 0, 0)),
                pl.BlockSpec((tokens, width), lambda i: (i, 0)),
            ),
            out_shape=(shape(clips, frames, places, width), shape(clips * tokens, width)),
            compiler_params=params(),
            cost_estimate=cost(clips * 4e9, spaced, qkv_time),
            name="time_attention",
        )(clip_start, by_place, gain_time, qkv_time, out_time)

        far = swap(unit, 2)
        units = [unit, swap(unit, 1), far, swap(far, 1)]
        chunk_tokens = clips * tokens

        def score(chunk_units):
            n = len(chunk_units)
            return simple_call(
                lambda *refs: score_kernel(*refs, blocks=blocks, chunks=n),
                (
                    shape(n, blocks * code_rows, chunk_tokens, dtype=BF16),
                    shape(n, 1, chunk_tokens),
                ),
                *code_blocks,
                *chunk_units,
                flops=n * 4 * blocks * code_rows * chunk_tokens * width,
                name="scores",
            )

        near_w, near_totals = score(units[:2])
        far_w, far_totals = score(units[2:])
        totals = [near_totals, far_totals]
        for m in range(1, sharers):
            totals += [swap(near_totals, m), swap(far_totals, m)]

        terms = simple_call(
            lambda *refs: term_kernel(*refs, blocks=blocks, chunks=sharers, calls=2),
            shape(blocks, code_rows + 8, width),
            near_w,
            far_w,
            *units,
            *totals,
            flops=2 * sharers * blocks * code_rows * chunk_tokens * width,
            name="terms",
        )
        arrived = [terms[0]] + [swap(terms[r], r * sharers) for r in range(1, blocks)]
        new_sums, new_counts, new_codebook = simple_call(
            lambda *refs: update_kernel(*refs, blocks=blocks),
            (shape(code_rows, width), shape(1, code_rows), shape(code_rows, width)),
            code_sums,
            counts_row,
            *arrived,
            name="update",
        )
        return (latents, new_sums, new_counts[0], new_codebook)

    return local


def solution(mesh):
    in_specs = (
        P("groups", "frames", None, None),
        P("groups"),
        P(),
        P(),
        P(),
        P(),
        P(),
        P(),
        P(("groups", "frames"), None),
        P(("groups", "frames")),
    )
    out_specs = (
        P("groups", None, "frames", None),
        P(("groups", "frames"), None),
        P(("groups", "frames")),
        P(("groups", "frames"), None),
    )
    local = make_local(mesh.shape["frames"])
    return jax.shard_map(local, mesh=mesh, in_specs=in_specs, out_specs=out_specs, check_vma=False)
```

```python
import math

import jax
import jax.numpy as jnp
from jax import lax
from jax.experimental import pallas as pl
from jax.experimental.pallas import tpu as pltpu
from jax.sharding import PartitionSpec as P

HEADS = 4
ATTN_SCALE = 10.0
SOFTMAX_WARMTH = 0.05
DECAY_RATE = 0.9
EPSILON = 1e-06
SHARERS = 4
VMEM_BYTES = 40 * 1024 * 1024
FIRST_VMEM_BYTES = 62 * 1024 * 1024
BF16 = jnp.bfloat16
F32 = jnp.float32


def params(limit=VMEM_BYTES):
    return pltpu.CompilerParams(vmem_limit_bytes=limit)


def split(x):
    high = x.astype(BF16)
    return high, (x - high.astype(F32)).astype(BF16)


def dot(a, b):
    return jnp.dot(a, b, preferred_element_type=F32)


def dot_t(a, b):
    return lax.dot_general(a, b, (((1,), (1,)), ((), ())), preferred_element_type=F32)


def dot3(a, b, product=dot):
    ah, al = a
    bh, bl = b
    return product(ah, bh) + (product(al, bh) + product(ah, bl))


def attend(x, gain, w_qkv, w_out, mask):
    tokens, width = x.shape
    head = width // HEADS
    h = x * lax.rsqrt(jnp.mean(x * x, -1, keepdims=True) + EPSILON) * gain
    packed = dot3(split(h), split(w_qkv))
    row_head = lax.broadcasted_iota(jnp.int32, (width, width), 0) // head
    lane_head = lax.broadcasted_iota(jnp.int32, (width, width), 1) // head
    same_head = (row_head == lane_head).astype(BF16)

    def unit_heads(v):
        high, low = split(v * v)
        return v * lax.rsqrt(dot(high, same_head) + dot(low, same_head) + EPSILON)

    q = split(unit_heads(packed[:, :width]) * ATTN_SCALE)
    k = split(unit_heads(packed[:, width : 2 * width]))
    v = split(packed[:, 2 * width :])
    lanes = lax.broadcasted_iota(jnp.int32, (tokens, width), 1) // head
    mixed = jnp.zeros((tokens, width), F32)
    for i in range(HEADS):
        mine = lanes == i
        qi = [jnp.where(mine, part, jnp.zeros_like(part)) for part in q]
        weights = jnp.exp(dot3(qi, k, dot_t))
        if mask is not None:
            weights = jnp.where(mask, weights, 0.0)
        vi = [jnp.where(mine, part, jnp.full_like(part, fill)) for part, fill in zip(v, (1.0, 0.0))]
        r = dot3(split(weights), vi)
        totals = jnp.concatenate([r[:, width // 2 :], r[:, : width // 2]], axis=1)
        mixed = jnp.where(mine, r / totals, mixed)
    return x + dot3(split(mixed), split(w_out))


def space_kernel(me_ref, x_ref, gain_ref, w_qkv_ref, w_out_ref, *rest):
    *out_refs, by_device = rest
    for f in range(x_ref.shape[0]):
        y = attend(x_ref[f], gain_ref[...], w_qkv_ref[...], w_out_ref[...], None)
        by_device[...] = y.reshape(by_device.shape)
        for r, out_ref in enumerate(out_refs):
            for m in range(SHARERS):
                out_ref[m, f] = by_device[me_ref[0] ^ (m + SHARERS * r)]


def first_kernel(me_ref, video, gain, w_qkv, w_out, sums, counts, codes_ref, *rest, blocks):
    out_refs, refs, (by_device, sem) = rest[:blocks], rest[blocks:-2], rest[-2:]
    sources = (sums, counts, video.at[0], gain, w_qkv, w_out)
    copies = [pltpu.make_async_copy(a, b, sem.at[i]) for i, (a, b) in enumerate(zip(sources, refs))]
    for copy in copies:
        copy.start()
    for copy in copies[:2]:
        copy.wait()
    sums, counts, x, gain, w_qkv, w_out = refs
    code_kernel(sums, counts, codes_ref)
    for copy in copies[2:]:
        copy.wait()
    space_kernel(me_ref, x, gain, w_qkv, w_out, *out_refs, by_device)


def merge_kernel(*refs, blocks):
    arrived, out_refs = refs[:blocks], refs[blocks:]
    for m, out_ref in enumerate(out_refs):
        for r in range(blocks):
            out_ref[r] = arrived[r][m]


def time_kernel(me_ref, start_ref, gain_ref, w_qkv_ref, w_out_ref, *rest, clip):
    x_refs, (latents_ref, unit_ref) = rest[:SHARERS], rest[-2:]
    blocks, local_frames, places, width = x_refs[0].shape
    group = blocks * local_frames * places
    tokens = SHARERS * group
    x = jnp.concatenate([ref[...].reshape(group, width) for ref in x_refs], axis=0)
    me, start = me_ref[0], start_ref[clip]

    def place_and_frame(index):
        slot = index // places
        place, frame, slot = index - slot * places, slot % local_frames, slot // local_frames
        sender = (slot // blocks + SHARERS * (slot % blocks)) ^ me
        return place, sender * local_frames + frame

    place, later = place_and_frame(lax.broadcasted_iota(jnp.int32, (tokens, 1), 0))
    other, earlier = place_and_frame(lax.broadcasted_iota(jnp.int32, (1, tokens), 1))
    mask = (place == other) & ((earlier == later) | ((earlier < later) & (earlier >= start)))
    y = attend(x, gain_ref[...], w_qkv_ref[...], w_out_ref[...], mask)
    unit_ref[...] = y * lax.rsqrt(jnp.sum(y * y, -1, keepdims=True) + EPSILON)
    for slot in range(SHARERS * blocks):
        sender = (slot // blocks + SHARERS * (slot % blocks)) ^ me
        for f in range(local_frames):
            row = (slot * local_frames + f) * places
            latents_ref[0, sender * local_frames + f] = y[row : row + places]


def column(row, lanes):
    return jnp.transpose(jnp.broadcast_to(row, (lanes, row.shape[1])))


def code_kernel(sums_ref, counts_ref, out_ref):
    book = sums_ref[...] / column(counts_ref[...], sums_ref.shape[1])
    unit = book * lax.rsqrt(jnp.sum(book * book, -1, keepdims=True) + EPSILON)
    out_ref[...] = unit * (math.log2(math.e) / SOFTMAX_WARMTH)


def score_kernel(*refs, blocks, chunks, before):
    codes, units = refs[:blocks], refs[blocks : blocks + chunks]
    w_ref, totals_ref = refs[-2:]
    rows = codes[0].shape[0]
    if before:
        totals_ref[:before] = refs[blocks + chunks][...]
    for j in range(chunks):
        u = units[j][...].astype(BF16)
        totals = None
        for r in range(blocks):
            high, low = split(codes[r][...])
            w = jnp.exp2(dot_t(high, u) + dot_t(low, u)).astype(BF16)
            w_ref[j, r * rows : (r + 1) * rows, :] = w
            part = jnp.sum(w.astype(F32), 0, keepdims=True)
            totals = part if totals is None else totals + part
        totals_ref[before + j] = totals


def term_kernel(*refs, blocks, clips):
    each = 2 + 2 * SHARERS
    out_refs = refs[each * clips :]
    width = refs[2].shape[1]
    rows = refs[0].shape[1] // blocks
    scaled, shares, ws = [], [], []
    for c in range(clips):
        near, far = refs[each * c : each * c + 2]
        units = refs[each * c + 2 : each * c + 2 + SHARERS]
        totals = refs[each * c + 2 + SHARERS : each * (c + 1)]
        for j in range(SHARERS):
            total = totals[0][j]
            for m in range(1, SHARERS):
                total = total + totals[m][j ^ m]
            share = 1.0 / total
            column_share = jnp.concatenate([column(share, 128)] * (width // 128), axis=1)
            scaled.append((units[j][...] * column_share).astype(BF16))
            high, low = split(share)
            index = lax.broadcasted_iota(jnp.int32, (16, share.shape[1]), 0)
            pair = jnp.where(index == 0, high.astype(F32), jnp.where(index == 1, low.astype(F32), 0.0))
            shares.append(pair.astype(BF16))
            ws.append((near, far)[j // 2].at[j % 2])
    for r in reversed(range(blocks)):
        pieces = out_refs[:1] if r == 0 else out_refs[1:2] if r == 1 else out_refs[2 * r - 2 : 2 * r]
        sums = jnp.zeros((rows, width), F32)
        counts = jnp.zeros((16, rows), F32)
        for w_ref, unit, share in zip(ws, scaled, shares):
            w = w_ref[r * rows : (r + 1) * rows, :]
            sums = sums + dot(w, unit)
            counts = counts + dot_t(share, w)
        counts = jnp.sum(counts, 0, keepdims=True)
        if rows < width:
            counts = jnp.concatenate([counts, jnp.zeros((1, width - rows), F32)], axis=1)
        term = jnp.concatenate([sums, jnp.broadcast_to(counts, (8, width))], axis=0)
        row = 0
        for piece in pieces:
            piece[...] = term[row : row + piece.shape[0]]
            row += piece.shape[0]


def update_kernel(*refs, arrivals):
    sums_ref, counts_ref = refs[:2]
    new_sums_ref, new_counts_ref, new_book_ref = refs[-3:]
    rows, width = sums_ref.shape
    refs, term = refs[2:-3], None
    for pieces in arrivals:
        part = jnp.concatenate([ref[...] for ref in refs[:pieces]], axis=0)
        refs = refs[pieces:]
        term = part if term is None else term + part
    sums = DECAY_RATE * sums_ref[...] + (1.0 - DECAY_RATE) * term[:rows]
    counts = DECAY_RATE * counts_ref[...] + (1.0 - DECAY_RATE) * term[rows : rows + 1, :rows]
    new_sums_ref[...] = sums
    new_counts_ref[...] = counts
    new_book_ref[...] = sums / column(counts, width)


def whole(a):
    return pl.BlockSpec(a.shape, lambda *_: (0,) * a.ndim)


def cost(flops, *arrays):
    return pl.CostEstimate(
        flops=int(flops), bytes_accessed=int(sum(a.size * a.dtype.itemsize for a in arrays)), transcendentals=0
    )


def shape(*dims, dtype=F32):
    return jax.ShapeDtypeStruct(dims, dtype)


def simple_call(kernel, outs, *args, flops=0, name=None):
    return pl.pallas_call(
        kernel,
        out_shape=outs,
        compiler_params=params(),
        cost_estimate=cost(flops, *args, *(outs if isinstance(outs, (tuple, list)) else [outs])),
        name=name,
    )(*args)


def make_local(devices):
    sharers, blocks = SHARERS, devices // SHARERS

    def swap(x, bits):
        return lax.ppermute(x, "frames", [(i, i ^ bits) for i in range(devices)])

    def local(
        video,
        clip_start,
        gain_space,
        qkv_space,
        out_space,
        gain_time,
        qkv_time,
        out_time,
        code_sums,
        code_counts,
    ):
        clips, local_frames, all_places, width = video.shape
        places = all_places // devices
        frames = local_frames * devices
        code_rows = code_sums.shape[0]
        tokens = frames * places
        gain_space, gain_time = gain_space[None], gain_time[None]
        counts_row = code_counts[None]
        me = lax.axis_index("frames").astype(jnp.int32)[None]
        sent = [shape(sharers, local_frames, places, width)] * blocks
        by_device = pltpu.VMEM((devices, places, width), F32)

        hbm = pl.BlockSpec(memory_space=pltpu.HBM)
        smem = pl.BlockSpec(memory_space=pltpu.SMEM)
        operands = (video, gain_space, qkv_space, out_space, code_sums, counts_row)
        held = (code_sums, counts_row, video[0], gain_space, qkv_space, out_space)
        codes, *first = pl.pallas_call(
            lambda *refs: first_kernel(*refs, blocks=blocks),
            in_specs=[smem] + [hbm] * len(operands),
            out_shape=[shape(code_rows, width)] + sent,
            scratch_shapes=[pltpu.VMEM(a.shape, a.dtype) for a in held]
            + [by_device, pltpu.SemaphoreType.DMA((len(held),))],
            compiler_params=params(FIRST_VMEM_BYTES),
            cost_estimate=cost(2e9, *held),
            name="first_space",
        )(me, *operands)

        spaced = [first]
        for c in range(1, clips):
            spaced.append(
                pl.pallas_call(
                    space_kernel,
                    grid=(1,),
                    in_specs=[
                        smem,
                        pl.BlockSpec((None, local_frames, all_places, width), lambda i, c=c: (c, 0, 0, 0)),
                        whole(gain_space),
                        whole(qkv_space),
                        whole(out_space),
                    ],
                    out_specs=[whole(a) for a in sent],
                    out_shape=sent,
                    scratch_shapes=[by_device],
                    compiler_params=params(),
                    cost_estimate=cost(2e9, *held),
                    name="space_attention",
                )(me, video, gain_space, qkv_space, out_space)
            )

        by_sender = []
        for c in range(clips):
            arrived = [spaced[c][0]] + [swap(spaced[c][r], r * sharers) for r in range(1, blocks)]
            merged = simple_call(
                lambda *refs: merge_kernel(*refs, blocks=blocks),
                [shape(blocks, local_frames, places, width)] * sharers,
                *arrived,
                name="merge",
            )
            if c == clips - 1:
                codes, *merged = lax.optimization_barrier((codes, *merged))
            by_sender.append([merged[0]] + [swap(merged[m], m) for m in range(1, sharers)])

        code_blocks = {0: codes}
        for bit in reversed(range((blocks - 1).bit_length())):
            step = 1 << bit
            code_blocks |= {r ^ step: swap(block, step * sharers) for r, block in code_blocks.items()}
        code_blocks = [code_blocks[r] for r in range(blocks)]

        latents = None
        units = []
        for c in range(clips):
            before = [] if latents is None else [latents]
            latents, unit = pl.pallas_call(
                lambda *refs, c=c: time_kernel(*refs, clip=c),
                grid=(1,),
                in_specs=[smem, smem, whole(gain_time), whole(qkv_time), whole(out_time)]
                + [whole(a) for a in by_sender[c]]
                + [pl.BlockSpec(memory_space=pl.ANY)] * len(before),
                out_specs=(
                    pl.BlockSpec((1, frames, places, width), lambda i, c=c: (c, 0, 0, 0)),
                    pl.BlockSpec((tokens, width), lambda i: (0, 0)),
                ),
                out_shape=(shape(clips, frames, places, width), shape(tokens, width)),
                input_output_aliases={5 + sharers: 0} if before else {},
                compiler_params=params(),
                cost_estimate=cost(2e9, *held),
                name="time_attention",
            )(me, clip_start, gain_time, qkv_time, out_time, *by_sender[c], *before)

            if units:
                unit, units[-1][2] = lax.optimization_barrier((unit, units[-1][2]))
            far = swap(unit, 2)
            units.append([unit, swap(unit, 1), far, swap(far, 1)])

        def score(chunk_units, *before):
            n, m = len(chunk_units), len(before) * 2
            return simple_call(
                lambda *refs: score_kernel(*refs, blocks=blocks, chunks=n, before=m),
                (shape(n, blocks * code_rows, tokens, dtype=BF16), shape(m + n, 1, tokens)),
                *code_blocks,
                *chunk_units,
                *before,
                flops=n * 4 * blocks * code_rows * tokens * width,
                name="scores",
            )

        operands = []
        for c in range(clips):
            if c:
                units[c][2], clip_totals = lax.optimization_barrier((units[c][2], clip_totals))
            near_w, near_totals = score(units[c][:2])
            far_w, clip_totals = score(units[c][2:], near_totals)
            operands += [near_w, far_w, *units[c], clip_totals]
            operands += [swap(clip_totals, m) for m in range(1, sharers)]

        half = code_rows // 2
        one, two = [shape(code_rows + 8, width)], [shape(half, width), shape(code_rows + 8 - half, width)]
        terms = simple_call(
            lambda *refs: term_kernel(*refs, blocks=blocks, clips=clips),
            one * 2 + two * (blocks - 2),
            *operands,
            flops=2 * sharers * blocks * code_rows * clips * tokens * width,
            name="terms",
        )
        terms = [[terms[0]], [terms[1]]] + [list(terms[2 * r - 2 : 2 * r]) for r in range(2, blocks)]

        arrivals = [terms[0]]
        for bit in range((blocks - 1).bit_length()):
            step = 1 << bit
            for r in reversed(range(step, blocks, 2 * step)):
                came = [swap(piece, step * sharers) for piece in terms[r]]
                if r == step:
                    arrivals.append(came)
                else:
                    terms[r - step] = [a + b for a, b in zip(terms[r - step], came)]
        new_sums, new_counts, new_codebook = simple_call(
            lambda *refs: update_kernel(*refs, arrivals=[len(pieces) for pieces in arrivals]),
            (shape(code_rows, width), shape(1, code_rows), shape(code_rows, width)),
            code_sums,
            counts_row,
            *[piece for pieces in arrivals for piece in pieces],
            name="update",
        )
        return (latents, new_sums, new_counts[0], new_codebook)

    return local


def solution(mesh):
    in_specs = (
        P("groups", "frames", None, None),
        P("groups"),
        P(),
        P(),
        P(),
        P(),
        P(),
        P(),
        P(("groups", "frames"), None),
        P(("groups", "frames")),
    )
    out_specs = (
        P("groups", None, "frames", None),
        P(("groups", "frames"), None),
        P(("groups", "frames")),
        P(("groups", "frames"), None),
    )
    local = make_local(mesh.shape["frames"])
    return jax.shard_map(local, mesh=mesh, in_specs=in_specs, out_specs=out_specs, check_vma=False)
```

```python
import math

import jax
import jax.numpy as jnp
from jax import lax
from jax.experimental import pallas as pl
from jax.experimental.pallas import tpu as pltpu
from jax.sharding import PartitionSpec as P

HEADS = 4
ATTN_SCALE = 10.0
SOFTMAX_WARMTH = 0.05
DECAY_RATE = 0.9
EPSILON = 1e-06
SHARERS = 4
VMEM_BYTES = 40 * 1024 * 1024
FIRST_VMEM_BYTES = 62 * 1024 * 1024
BF16 = jnp.bfloat16
F32 = jnp.float32


def params(limit=VMEM_BYTES):
    return pltpu.CompilerParams(vmem_limit_bytes=limit)


def split(x):
    high = x.astype(BF16)
    return high, (x - high.astype(F32)).astype(BF16)


def dot(a, b):
    return jnp.dot(a, b, preferred_element_type=F32)


def dot_t(a, b):
    return lax.dot_general(a, b, (((1,), (1,)), ((), ())), preferred_element_type=F32)


def dot3(a, b, product=dot):
    ah, al = a
    bh, bl = b
    return product(ah, bh) + (product(al, bh) + product(ah, bl))


def attend(x, gain, w_qkv, w_out, mask):
    tokens, width = x.shape
    head = width // HEADS
    h = x * lax.rsqrt(jnp.mean(x * x, -1, keepdims=True) + EPSILON) * gain
    packed = dot3(split(h), w_qkv)
    row_head = lax.broadcasted_iota(jnp.int32, (width, width), 0) // head
    lane_head = lax.broadcasted_iota(jnp.int32, (width, width), 1) // head
    same_head = (row_head == lane_head).astype(BF16)

    def unit_heads(v):
        high, low = split(v * v)
        return v * lax.rsqrt(dot(high, same_head) + dot(low, same_head) + EPSILON)

    q = split(unit_heads(packed[:, :width]) * ATTN_SCALE)
    k = split(unit_heads(packed[:, width : 2 * width]))
    v = split(packed[:, 2 * width :])
    lanes = lax.broadcasted_iota(jnp.int32, (tokens, width), 1) // head
    sums = totals = None
    for i in range(HEADS):
        mine = lanes == i
        qi = [jnp.where(mine, part, jnp.zeros_like(part)) for part in q]
        weights = jnp.exp(dot3(qi, k, dot_t))
        if mask is not None:
            weights = jnp.where(mask, weights, 0.0)
        vi = [jnp.where(mine, part, jnp.full_like(part, fill)) for part, fill in zip(v, (1.0, 0.0))]
        r = dot3(split(weights), vi)
        sums = r if i == 0 else jnp.where(mine, r, sums)
        totals = r if i == 0 else jnp.where(lanes == (i + HEADS // 2) % HEADS, r, totals)
    totals = jnp.concatenate([totals[:, width // 2 :], totals[:, : width // 2]], axis=1)
    return x + dot3(split(sums / totals), w_out)


def first_kernel(video, gain, w_qkv, w_out, sums, counts, codes_ref, out_ref, *scratch):
    refs, sem = scratch[:-1], scratch[-1]
    sources = (sums, counts, video, gain, w_qkv, w_out)
    copies = [pltpu.make_async_copy(a, b, sem.at[i]) for i, (a, b) in enumerate(zip(sources, refs))]
    for copy in copies:
        copy.start()
    for copy in copies[:2]:
        copy.wait()
    sums, counts, x, gain, w_qkv, w_out = refs
    code_kernel(sums, counts, codes_ref)
    for copy in copies[2:]:
        copy.wait()
    clips, local_frames = x.shape[:2]
    places, width = out_ref.shape[2:]
    w_qkv, w_out = split(w_qkv[...]), split(w_out[...])
    for c in range(clips):
        for f in range(local_frames):
            y = attend(x[c, f], gain[...], w_qkv, w_out, None)
            out_ref[:, c * local_frames + f] = y.reshape(-1, places, width)


def time_kernel(start_ref, x_ref, gain_ref, w_qkv_ref, w_out_ref, *rest, clip):
    latents_ref, unit_ref = rest[-2:]
    senders, _, local_frames, places, width = x_ref.shape
    tokens = senders * local_frames * places
    x = x_ref[...].reshape(tokens, width)
    row = lax.broadcasted_iota(jnp.int32, (tokens, 1), 0)
    col = lax.broadcasted_iota(jnp.int32, (1, tokens), 1)
    later, earlier = row // places, col // places
    mask = ((row - later * places) == (col - earlier * places)) & (
        (earlier == later) | ((earlier < later) & (earlier >= start_ref[clip]))
    )
    y = attend(x, gain_ref[...], split(w_qkv_ref[...]), split(w_out_ref[...]), mask)
    latents_ref[...] = y.reshape(latents_ref.shape)
    unit_ref[...] = y * lax.rsqrt(jnp.sum(y * y, -1, keepdims=True) + EPSILON)


def column(row, lanes):
    return jnp.transpose(jnp.broadcast_to(row, (lanes, row.shape[1])))


def code_kernel(sums_ref, counts_ref, out_ref):
    book = sums_ref[...] / column(counts_ref[...], sums_ref.shape[1])
    unit = book * lax.rsqrt(jnp.sum(book * book, -1, keepdims=True) + EPSILON)
    out_ref[...] = unit * (math.log2(math.e) / SOFTMAX_WARMTH)


def score_kernel(*refs, blocks, chunks, before):
    codes, units = refs[:blocks], refs[blocks : blocks + chunks]
    w_ref, totals_ref = refs[-2:]
    rows = codes[0].shape[0]
    if before:
        totals_ref[:before] = refs[blocks + chunks][...]
    for j in range(chunks):
        u = units[j][...].astype(BF16)
        totals = None
        for r in range(blocks):
            high, low = split(codes[r][...])
            w = jnp.exp2(dot_t(high, u) + dot_t(low, u)).astype(BF16)
            w_ref[j, r * rows : (r + 1) * rows, :] = w
            part = jnp.sum(w.astype(F32), 0, keepdims=True)
            totals = part if totals is None else totals + part
        totals_ref[before + j] = totals


def term_kernel(*refs, blocks, clips):
    each = 2 + 2 * SHARERS
    out_refs = refs[each * clips :]
    width = refs[2].shape[1]
    rows = refs[0].shape[1] // blocks
    scaled, shares, ws = [], [], []
    for c in range(clips):
        near, far = refs[each * c : each * c + 2]
        units = refs[each * c + 2 : each * c + 2 + SHARERS]
        totals = refs[each * c + 2 + SHARERS : each * (c + 1)]
        for j in range(SHARERS):
            total = totals[0][j]
            for m in range(1, SHARERS):
                total = total + totals[m][j ^ m]
            share = 1.0 / total
            column_share = jnp.concatenate([column(share, 128)] * (width // 128), axis=1)
            scaled.append((units[j][...] * column_share).astype(BF16))
            high, low = split(share)
            index = lax.broadcasted_iota(jnp.int32, (16, share.shape[1]), 0)
            pair = jnp.where(index == 0, high.astype(F32), jnp.where(index == 1, low.astype(F32), 0.0))
            shares.append(pair.astype(BF16))
            ws.append((near, far)[j // 2].at[j % 2])
    for r in reversed(range(blocks)):
        pieces = out_refs[:1] if r == 0 else out_refs[1:2] if r == 1 else out_refs[2 * r - 2 : 2 * r]
        sums = jnp.zeros((rows, width), F32)
        counts = jnp.zeros((16, rows), F32)
        for w_ref, unit, share in zip(ws, scaled, shares):
            w = w_ref[r * rows : (r + 1) * rows, :]
            sums = sums + dot(w, unit)
            counts = counts + dot_t(share, w)
        counts = jnp.sum(counts, 0, keepdims=True)
        if rows < width:
            counts = jnp.concatenate([counts, jnp.zeros((1, width - rows), F32)], axis=1)
        term = jnp.concatenate([sums, jnp.broadcast_to(counts, (8, width))], axis=0)
        row = 0
        for piece in pieces:
            piece[...] = term[row : row + piece.shape[0]]
            row += piece.shape[0]


def update_kernel(*refs, arrivals):
    sums_ref, counts_ref = refs[:2]
    new_sums_ref, new_counts_ref, new_book_ref = refs[-3:]
    rows, width = sums_ref.shape
    refs, term = refs[2:-3], None
    for pieces in arrivals:
        part = jnp.concatenate([ref[...] for ref in refs[:pieces]], axis=0)
        refs = refs[pieces:]
        term = part if term is None else term + part
    sums = DECAY_RATE * sums_ref[...] + (1.0 - DECAY_RATE) * term[:rows]
    counts = DECAY_RATE * counts_ref[...] + (1.0 - DECAY_RATE) * term[rows : rows + 1, :rows]
    new_sums_ref[...] = sums
    new_counts_ref[...] = counts
    new_book_ref[...] = sums / column(counts, width)


def whole(a):
    return pl.BlockSpec(a.shape, lambda *_: (0,) * a.ndim)


def cost(flops, *arrays):
    return pl.CostEstimate(
        flops=int(flops), bytes_accessed=int(sum(a.size * a.dtype.itemsize for a in arrays)), transcendentals=0
    )


def shape(*dims, dtype=F32):
    return jax.ShapeDtypeStruct(dims, dtype)


def simple_call(kernel, outs, *args, flops=0, name=None):
    return pl.pallas_call(
        kernel,
        out_shape=outs,
        compiler_params=params(),
        cost_estimate=cost(flops, *args, *(outs if isinstance(outs, (tuple, list)) else [outs])),
        name=name,
    )(*args)


def make_local(devices):
    sharers, blocks = SHARERS, devices // SHARERS
    sharer_bits = [(m & 1) | (m >> 1) << 2 for m in range(sharers)]
    block_bits = [(r & 1) << 1 | (r >> 1) << 3 for r in range(blocks)]

    def swap(x, bits):
        return lax.ppermute(x, "frames", [(i, i ^ bits) for i in range(devices)])

    def local(
        video,
        clip_start,
        gain_space,
        qkv_space,
        out_space,
        gain_time,
        qkv_time,
        out_time,
        code_sums,
        code_counts,
    ):
        clips, local_frames, all_places, width = video.shape
        places = all_places // devices
        frames = local_frames * devices
        code_rows = code_sums.shape[0]
        tokens = frames * places
        gain_space, gain_time = gain_space[None], gain_time[None]
        counts_row = code_counts[None]

        hbm = pl.BlockSpec(memory_space=pltpu.HBM)
        operands = (video, gain_space, qkv_space, out_space, code_sums, counts_row)
        held = (code_sums, counts_row, video, gain_space, qkv_space, out_space)
        codes, spaced = pl.pallas_call(
            first_kernel,
            in_specs=[hbm] * len(operands),
            out_shape=[shape(code_rows, width), shape(devices, clips * local_frames, places, width)],
            scratch_shapes=[pltpu.VMEM(a.shape, a.dtype) for a in held]
            + [pltpu.SemaphoreType.DMA((len(held),))],
            compiler_params=params(FIRST_VMEM_BYTES),
            cost_estimate=cost(clips * 2e9, *held),
            name="first_space",
        )(*operands)

        by_place = lax.all_to_all(spaced, "frames", split_axis=0, concat_axis=0, tiled=True)
        codes, by_place = lax.optimization_barrier((codes, by_place))
        by_place = by_place.reshape(devices, clips, local_frames, places, width)

        half = code_rows // 2
        halves = {0: [codes[:half], codes[half:]]}
        for bit in reversed(range((blocks - 1).bit_length())):
            step = 1 << bit
            halves |= {r ^ step: [swap(part, block_bits[step]) for part in block] for r, block in halves.items()}
        code_blocks = [part for r in range(blocks) for part in halves[r]]

        latents = None
        units = []
        for c in range(clips):
            before = [] if latents is None else [latents]
            latents, unit = pl.pallas_call(
                lambda *refs, c=c: time_kernel(*refs, clip=c),
                grid=(1,),
                in_specs=[
                    pl.BlockSpec(memory_space=pltpu.SMEM),
                    pl.BlockSpec((devices, 1, local_frames, places, width), lambda i, c=c: (0, c, 0, 0, 0)),
                    whole(gain_time),
                    whole(qkv_time),
                    whole(out_time),
                ]
                + [pl.BlockSpec(memory_space=pl.ANY)] * len(before),
                out_specs=(
                    pl.BlockSpec((1, frames, places, width), lambda i, c=c: (c, 0, 0, 0)),
                    pl.BlockSpec((tokens, width), lambda i: (0, 0)),
                ),
                out_shape=(shape(clips, frames, places, width), shape(tokens, width)),
                input_output_aliases={5: 0} if before else {},
                compiler_params=params(),
                cost_estimate=cost(2e9, *held),
                name="time_attention",
            )(clip_start, by_place, gain_time, qkv_time, out_time, *before)

            if units:
                unit, units[-1][2] = lax.optimization_barrier((unit, units[-1][2]))
            far = swap(unit, sharer_bits[2])
            units.append([unit, swap(unit, 1), far, swap(far, 1)])

        def score(chunk_units, *before):
            n, m = len(chunk_units), len(before) * 2
            return simple_call(
                lambda *refs: score_kernel(*refs, blocks=2 * blocks, chunks=n, before=m),
                (shape(n, blocks * code_rows, tokens, dtype=BF16), shape(m + n, 1, tokens)),
                *code_blocks,
                *chunk_units,
                *before,
                flops=n * 4 * blocks * code_rows * tokens * width,
                name="scores",
            )

        operands = []
        for c in range(clips):
            if c:
                units[c][2], clip_totals = lax.optimization_barrier((units[c][2], clip_totals))
            near_w, near_totals = score(units[c][:2])
            far_w, clip_totals = score(units[c][2:], near_totals)
            operands += [near_w, far_w, *units[c], clip_totals]
            operands += [swap(clip_totals, sharer_bits[m]) for m in range(1, sharers)]

        half = code_rows // 2
        one, two = [shape(code_rows + 8, width)], [shape(half, width), shape(code_rows + 8 - half, width)]
        terms = simple_call(
            lambda *refs: term_kernel(*refs, blocks=blocks, clips=clips),
            one * 2 + two * (blocks - 2),
            *operands,
            flops=2 * sharers * blocks * code_rows * clips * tokens * width,
            name="terms",
        )
        terms = [[terms[0]], [terms[1]]] + [list(terms[2 * r - 2 : 2 * r]) for r in range(2, blocks)]

        arrivals = [terms[0]]
        for bit in range((blocks - 1).bit_length()):
            step = 1 << bit
            for r in reversed(range(step, blocks, 2 * step)):
                came = [swap(piece, block_bits[step]) for piece in terms[r]]
                if r == step:
                    arrivals.append(came)
                else:
                    terms[r - step] = [a + b for a, b in zip(terms[r - step], came)]
        new_sums, new_counts, new_codebook = simple_call(
            lambda *refs: update_kernel(*refs, arrivals=[len(pieces) for pieces in arrivals]),
            (shape(code_rows, width), shape(1, code_rows), shape(code_rows, width)),
            code_sums,
            counts_row,
            *[piece for pieces in arrivals for piece in pieces],
            name="update",
        )
        return (latents, new_sums, new_counts[0], new_codebook)

    return local


def solution(mesh):
    in_specs = (
        P("groups", "frames", None, None),
        P("groups"),
        P(),
        P(),
        P(),
        P(),
        P(),
        P(),
        P(("groups", "frames"), None),
        P(("groups", "frames")),
    )
    out_specs = (
        P("groups", None, "frames", None),
        P(("groups", "frames"), None),
        P(("groups", "frames")),
        P(("groups", "frames"), None),
    )
    local = make_local(mesh.shape["frames"])
    return jax.shard_map(local, mesh=mesh, in_specs=in_specs, out_specs=out_specs, check_vma=False)
```

```python
import math

import jax
import jax.numpy as jnp
from jax import lax
from jax.experimental import pallas as pl
from jax.experimental.pallas import tpu as pltpu
from jax.sharding import PartitionSpec as P

HEADS = 4
ATTN_SCALE = 10.0
SOFTMAX_WARMTH = 0.05
DECAY_RATE = 0.9
EPSILON = 1e-06
SHARERS = 4
VMEM_BYTES = 40 * 1024 * 1024
FIRST_VMEM_BYTES = 62 * 1024 * 1024
BF16 = jnp.bfloat16
F32 = jnp.float32


def params(limit=VMEM_BYTES):
    return pltpu.CompilerParams(vmem_limit_bytes=limit)


def split(x):
    high = x.astype(BF16)
    return high, (x - high.astype(F32)).astype(BF16)


def dot(a, b):
    return jnp.dot(a, b, preferred_element_type=F32)


def dot_t(a, b):
    return lax.dot_general(a, b, (((1,), (1,)), ((), ())), preferred_element_type=F32)


def dot3(a, b, product=dot):
    ah, al = a
    bh, bl = b
    return product(ah, bh) + (product(al, bh) + product(ah, bl))


def attend(x, gain, w_qkv, w_out, mask):
    tokens, width = x.shape
    head = width // HEADS
    h = x * lax.rsqrt(jnp.mean(x * x, -1, keepdims=True) + EPSILON) * gain
    packed = dot3(split(h), w_qkv)
    row_head = lax.broadcasted_iota(jnp.int32, (width, width), 0) // head
    lane_head = lax.broadcasted_iota(jnp.int32, (width, width), 1) // head
    same_head = (row_head == lane_head).astype(BF16)

    def unit_heads(v):
        high, low = split(v * v)
        return v * lax.rsqrt(dot(high, same_head) + dot(low, same_head) + EPSILON)

    q = split(unit_heads(packed[:, :width]) * ATTN_SCALE)
    k = split(unit_heads(packed[:, width : 2 * width]))
    v = split(packed[:, 2 * width :])
    lanes = lax.broadcasted_iota(jnp.int32, (tokens, width), 1) // head
    sums = totals = None
    for i in range(HEADS):
        mine = lanes == i
        qi = [jnp.where(mine, part, jnp.zeros_like(part)) for part in q]
        weights = jnp.exp(dot3(qi, k, dot_t))
        if mask is not None:
            weights = jnp.where(mask, weights, 0.0)
        vi = [jnp.where(mine, part, jnp.full_like(part, fill)) for part, fill in zip(v, (1.0, 0.0))]
        r = dot3(split(weights), vi)
        sums = r if i == 0 else jnp.where(mine, r, sums)
        totals = r if i == 0 else jnp.where(lanes == (i + HEADS // 2) % HEADS, r, totals)
    totals = jnp.concatenate([totals[:, width // 2 :], totals[:, : width // 2]], axis=1)
    return x + dot3(split(sums / totals), w_out)


def first_kernel(*refs, names):
    sources = dict(zip(names, refs))
    codes_ref, out_ref, start_ref, gain_ref, *weight_refs = refs[len(names) : -len(names) - 1]
    held, sem = dict(zip(names, refs[-len(names) - 1 : -1])), refs[-1]
    copies = {n: pltpu.make_async_copy(sources[n], held[n], sem.at[i]) for i, n in enumerate(names)}
    for copy in copies.values():
        copy.start()

    def take(*wanted):
        for n in wanted:
            copies[n].wait()
        return [held[n] for n in wanted]

    code_kernel(*take("code_sums", "code_counts"), codes_ref)
    x, gain, w_qkv, w_out = take("video", "gain_space", "qkv_space", "out_space")
    clips, local_frames = x.shape[:2]
    places, width = out_ref.shape[2:]
    w_qkv, w_out = split(w_qkv[...]), split(w_out[...])
    for c in range(clips):
        for f in range(local_frames):
            y = attend(x[c, f], gain[...], w_qkv, w_out, None)
            out_ref[:, c * local_frames + f] = y.reshape(-1, places, width)
    start, gain, w_qkv, w_out = take("clip_start", "gain_time", "qkv_time", "out_time")
    for c in range(clips):
        start_ref[c] = jnp.full(start_ref.shape[1:], start[c], jnp.int32)
    gain_ref[...] = gain[...]
    for ref, part in zip(weight_refs, split(w_qkv[...]) + split(w_out[...])):
        ref[...] = part


def time_kernel(start_ref, x_ref, gain_ref, *refs, clip):
    weights, (latents_ref, unit_ref) = [ref[...] for ref in refs[:4]], refs[-2:]
    senders, _, local_frames, places, width = x_ref.shape
    tokens = senders * local_frames * places
    x = x_ref[:, clip].reshape(tokens, width)
    row = lax.broadcasted_iota(jnp.int32, (tokens, 1), 0)
    col = lax.broadcasted_iota(jnp.int32, (1, tokens), 1)
    later, earlier = row // places, col // places
    mask = ((row - later * places) == (col - earlier * places)) & (
        (earlier == later) | ((earlier < later) & (earlier >= start_ref[clip, :1, :1]))
    )
    y = attend(x, gain_ref[...], weights[:2], weights[2:], mask)
    unit_ref[...] = y * lax.rsqrt(jnp.sum(y * y, -1, keepdims=True) + EPSILON)
    for i, ref in enumerate(refs[4:-2]):
        latents_ref[i] = ref[...]
    y = y.reshape(latents_ref.shape[-3:])
    if latents_ref.ndim == 4:
        latents_ref[clip] = y
    else:
        latents_ref[...] = y


def column(row, lanes):
    return jnp.transpose(jnp.broadcast_to(row, (lanes, row.shape[1])))


def code_kernel(sums_ref, counts_ref, out_ref):
    book = sums_ref[...] / column(counts_ref[...], sums_ref.shape[1])
    unit = book * lax.rsqrt(jnp.sum(book * book, -1, keepdims=True) + EPSILON)
    out_ref[...] = unit * (math.log2(math.e) / SOFTMAX_WARMTH)


def score_kernel(*refs, blocks, chunks, before):
    codes, units = refs[:blocks], refs[blocks : blocks + chunks]
    w_ref, totals_ref = refs[-2:]
    rows = codes[0].shape[0]
    if before:
        totals_ref[:before] = refs[blocks + chunks][...]
    for j in range(chunks):
        u = units[j][...].astype(BF16)
        totals = None
        for r in range(blocks):
            high, low = split(codes[r][...])
            w = jnp.exp2(dot_t(high, u) + dot_t(low, u)).astype(BF16)
            w_ref[j, r * rows : (r + 1) * rows, :] = w
            part = jnp.sum(w.astype(F32), 0, keepdims=True)
            totals = part if totals is None else totals + part
        totals_ref[before + j] = totals


def term_kernel(*refs, blocks, clips, which):
    each = 2 + 2 * SHARERS
    out_refs = refs[each * clips :]
    width = refs[2].shape[1]
    rows = refs[0].shape[1] // blocks
    scaled, shares, ws = [], [], []
    for c in range(clips):
        near, far = refs[each * c : each * c + 2]
        units = refs[each * c + 2 : each * c + 2 + SHARERS]
        totals = refs[each * c + 2 + SHARERS : each * (c + 1)]
        for j in range(SHARERS):
            total = totals[0][j]
            for m in range(1, SHARERS):
                total = total + totals[m][j ^ m]
            share = 1.0 / total
            column_share = jnp.concatenate([column(share, 128)] * (width // 128), axis=1)
            scaled.append((units[j][...] * column_share).astype(BF16))
            high, low = split(share)
            index = lax.broadcasted_iota(jnp.int32, (16, share.shape[1]), 0)
            pair = jnp.where(index == 0, high.astype(F32), jnp.where(index == 1, low.astype(F32), 0.0))
            shares.append(pair.astype(BF16))
            ws.append((near, far)[j // 2].at[j % 2])
    for r in which:
        pieces, out_refs = out_refs[: 1 + (r > 1)], out_refs[1 + (r > 1) :]
        sums = jnp.zeros((rows, width), F32)
        counts = jnp.zeros((16, rows), F32)
        for w_ref, unit, share in zip(ws, scaled, shares):
            w = w_ref[r * rows : (r + 1) * rows, :]
            sums = sums + dot(w, unit)
            counts = counts + dot_t(share, w)
        counts = jnp.sum(counts, 0, keepdims=True)
        if rows < width:
            counts = jnp.concatenate([counts, jnp.zeros((1, width - rows), F32)], axis=1)
        term = jnp.concatenate([sums, jnp.broadcast_to(counts, (8, width))], axis=0)
        row = 0
        for piece in pieces:
            piece[...] = term[row : row + piece.shape[0]]
            row += piece.shape[0]


def update_kernel(*refs, arrivals):
    sums_ref, counts_ref = refs[:2]
    new_sums_ref, new_counts_ref, new_book_ref = refs[-3:]
    rows, width = sums_ref.shape
    refs, term = refs[2:-3], None
    for pieces in arrivals:
        part = jnp.concatenate([ref[...] for ref in refs[:pieces]], axis=0)
        refs = refs[pieces:]
        term = part if term is None else term + part
    sums = DECAY_RATE * sums_ref[...] + (1.0 - DECAY_RATE) * term[:rows]
    counts = DECAY_RATE * counts_ref[...] + (1.0 - DECAY_RATE) * term[rows : rows + 1, :rows]
    new_sums_ref[...] = sums
    new_counts_ref[...] = counts
    new_book_ref[...] = sums / column(counts, width)


def whole(a):
    return pl.BlockSpec(a.shape, lambda *_: (0,) * a.ndim)


def cost(flops, *arrays):
    return pl.CostEstimate(
        flops=int(flops), bytes_accessed=int(sum(a.size * a.dtype.itemsize for a in arrays)), transcendentals=0
    )


def shape(*dims, dtype=F32):
    return jax.ShapeDtypeStruct(dims, dtype)


def simple_call(kernel, outs, *args, flops=0, name=None):
    return pl.pallas_call(
        kernel,
        out_shape=outs,
        compiler_params=params(),
        cost_estimate=cost(flops, *args, *(outs if isinstance(outs, (tuple, list)) else [outs])),
        name=name,
    )(*args)


def make_local(devices):
    sharers, blocks = SHARERS, devices // SHARERS
    sharer_bits = [(m & 1) | (m >> 1) << 2 for m in range(sharers)]
    block_bits = [(r & 1) << 1 | (r >> 1) << 3 for r in range(blocks)]

    def swap(x, bits):
        return lax.ppermute(x, "frames", [(i, i ^ bits) for i in range(devices)])

    def local(
        video,
        clip_start,
        gain_space,
        qkv_space,
        out_space,
        gain_time,
        qkv_time,
        out_time,
        code_sums,
        code_counts,
    ):
        clips, local_frames, all_places, width = video.shape
        places = all_places // devices
        frames = local_frames * devices
        code_rows = code_sums.shape[0]
        tokens = frames * places
        gain_space, gain_time = gain_space[None], gain_time[None]
        counts_row = code_counts[None]

        hbm = pl.BlockSpec(memory_space=pltpu.HBM)
        operands = {
            "code_sums": code_sums,
            "code_counts": counts_row,
            "video": video,
            "gain_space": gain_space,
            "qkv_space": qkv_space,
            "out_space": out_space,
            "clip_start": clip_start,
            "gain_time": gain_time,
            "qkv_time": qkv_time,
            "out_time": out_time,
        }
        codes, spaced, *time_operands = pl.pallas_call(
            lambda *refs: first_kernel(*refs, names=list(operands)),
            in_specs=[hbm] * len(operands),
            out_shape=[
                shape(code_rows, width),
                shape(devices, clips * local_frames, places, width),
                shape(clips, 8, 128, dtype=jnp.int32),
                shape(1, width),
            ]
            + [shape(*w.shape, dtype=BF16) for w in (qkv_time, qkv_time, out_time, out_time)],
            scratch_shapes=[
                (pltpu.SMEM if name == "clip_start" else pltpu.VMEM)(a.shape, a.dtype)
                for name, a in operands.items()
            ]
            + [pltpu.SemaphoreType.DMA((len(operands),))],
            compiler_params=params(FIRST_VMEM_BYTES),
            cost_estimate=cost(clips * 2e9, *operands.values()),
            name="first_space",
        )(*operands.values())
        start, gain, *weights = time_operands

        code_blocks = {0: codes}
        for bit in reversed(range((blocks - 1).bit_length())):
            step = 1 << bit
            code_blocks |= {r ^ step: swap(block, block_bits[step]) for r, block in code_blocks.items()}

        by_place = lax.all_to_all(spaced, "frames", split_axis=0, concat_axis=0, tiled=True)
        if blocks > 2:
            by_place, code_blocks[2] = lax.optimization_barrier((by_place, code_blocks[2]))
        by_place = by_place.reshape(devices, clips, local_frames, places, width)
        code_blocks = [code_blocks[r] for r in range(blocks)]

        latents = []
        units = []
        for c in range(clips):
            last = c == clips - 1
            of_clip, unit = simple_call(
                lambda *refs, c=c: time_kernel(*refs, clip=c),
                (shape(*([clips] * last), frames, places, width), shape(tokens, width)),
                start,
                by_place,
                gain,
                *weights,
                *(latents if last else []),
                flops=2e9,
                name="time_attention",
            )
            latents.append(of_clip)

            if units:
                unit, units[-1][2] = lax.optimization_barrier((unit, units[-1][2]))
            far = swap(unit, sharer_bits[2])
            units.append([unit, swap(unit, 1), far, swap(far, 1)])
        latents = latents[-1]

        def score(chunk_units, *before):
            n, m = len(chunk_units), len(before) * 2
            return simple_call(
                lambda *refs: score_kernel(*refs, blocks=blocks, chunks=n, before=m),
                (shape(n, blocks * code_rows, tokens, dtype=BF16), shape(m + n, 1, tokens)),
                *code_blocks,
                *chunk_units,
                *before,
                flops=n * 4 * blocks * code_rows * tokens * width,
                name="scores",
            )

        operands = []
        for c in range(clips):
            if c:
                units[c][2], clip_totals = lax.optimization_barrier((units[c][2], clip_totals))
            near_w, near_totals = score(units[c][:2])
            far_w, clip_totals = score(units[c][2:], near_totals)
            operands += [near_w, far_w, *units[c], clip_totals]
            operands += [swap(clip_totals, sharer_bits[m]) for m in range(1, sharers)]

        half = code_rows // 2
        whole_term, pieces = [shape(code_rows + 8, width)], [shape(half, width), shape(code_rows + 8 - half, width)]
        terms = {}
        for which in ([blocks - 1], list(reversed(range(blocks - 1)))):
            made = simple_call(
                lambda *refs, which=which: term_kernel(*refs, blocks=blocks, clips=clips, which=which),
                [a for r in which for a in (pieces if r > 1 else whole_term)],
                *operands,
                flops=2 * sharers * len(which) * code_rows * clips * tokens * width,
                name="terms",
            )
            for r in which:
                terms[r], made = list(made[: 1 + (r > 1)]), made[1 + (r > 1) :]

        arrivals = []
        for bit in range((blocks - 1).bit_length()):
            step = 1 << bit
            ahead = None
            for r in reversed(range(step, blocks, 2 * step)):
                came = []
                for piece in terms[r]:
                    if ahead is not None:
                        piece, ahead, terms[0][0] = lax.optimization_barrier((piece, ahead, terms[0][0]))
                        came[-1:] = [ahead] if came else []
                    ahead = swap(piece, block_bits[step])
                    came.append(ahead)
                if r == step:
                    arrivals.append(came)
                else:
                    terms[r - step] = [a + b for a, b in zip(terms[r - step], came)]
        arrivals.insert(0, terms[0])
        new_sums, new_counts, new_codebook = simple_call(
            lambda *refs: update_kernel(*refs, arrivals=[len(pieces) for pieces in arrivals]),
            (shape(code_rows, width), shape(1, code_rows), shape(code_rows, width)),
            code_sums,
            counts_row,
            *[piece for pieces in arrivals for piece in pieces],
            name="update",
        )
        return (latents, new_sums, new_counts[0], new_codebook)

    return local


def solution(mesh):
    in_specs = (
        P("groups", "frames", None, None),
        P("groups"),
        P(),
        P(),
        P(),
        P(),
        P(),
        P(),
        P(("groups", "frames"), None),
        P(("groups", "frames")),
    )
    out_specs = (
        P("groups", None, "frames", None),
        P(("groups", "frames"), None),
        P(("groups", "frames")),
        P(("groups", "frames"), None),
    )
    local = make_local(mesh.shape["frames"])
    return jax.shard_map(local, mesh=mesh, in_specs=in_specs, out_specs=out_specs, check_vma=False)
```
